512 devices in a mesh: clip: 32 (over x, z), seq: 16 (over y, core).
Axes of the slice: x: 4, y: 8, z: 8, core: 2. Of those that a mesh axis runs over, the one named last changes fastest.
Arguments:
- queries: bfloat16 [65536, 4096], P(('clip', 'seq')), parts along dimension 0, may hold values from -8 to 8
- keys_in: bfloat16 [65536, 4096], P(('clip', 'seq')), parts along dimension 0, may hold values from -8 to 8
- value_input: bfloat16 [65536, 4096], P(('clip', 'seq')), parts along dimension 0, may hold values from -6 to 6
- head_class: int32 [1024], P('clip'), parts along dimension 0, may hold values from 0 to 1, as said below
- block_lists: int32 [1024, 16, 4], P('clip'), parts along dimension 0, may hold values from 0 to 15, as said below
Outputs:
- attended: bfloat16 [65536, 4096], P(('clip', 'seq')), parts along dimension 0
The draws below stay inside these ranges and needn't reach their ends.
There are 32 independent parts, one for each index of `clip`. The reference program is written for one: setup_inputs(seed, part) draws one part's arguments, and reference() takes and returns one part's arrays. A program takes and returns all parts, laid end to end along the dimension named above; each array names one. Nothing has to cross between parts.
Inputs may be any that keep to these rules, and one draw needn't show every extreme that they name: `head_class`: exactly 8 heads have class 1. Each row block_lists[h, i, :] holds 4 different block numbers, one of them i itself.
All inputs are finite; a program needn't handle non-finite values.
Results may differ from the reference program's by a relative error of at most 0.0046.
Values may be sent and summed in bfloat16 or wider, within the bound.
A program may use at most 64 MiB of HBM per device.

```python
import math
import jax
import jax.numpy as jnp
from jax import lax

HEADS = 32
HEAD_DIM = 128
BLOCK_LEN = 128
KSEL = 4
TOKENS = 2048
NB = 16


def draw_queries(key, part):
    key = jax.random.fold_in(key, 11)
    base = jnp.clip(jax.random.normal(key, (TOKENS, HEADS * HEAD_DIM), jnp.float32), -6.0, 6.0)
    return base.astype(jnp.bfloat16)


def draw_keys_in(key, part):
    key = jax.random.fold_in(key, 12)
    base = jnp.clip(jax.random.normal(key, (TOKENS, HEADS * HEAD_DIM), jnp.float32), -6.0, 6.0)
    return base.astype(jnp.bfloat16)


def draw_head_class(key, part):
    key = jax.random.fold_in(key, 13)
    shuffled = jax.random.permutation(key, HEADS)
    return (shuffled < HEADS // 4).astype(jnp.int32)


def draw_block_lists(key, part):
    key = jax.random.fold_in(key, 14)
    raw = jax.random.randint(key, (HEADS, NB, NB), 0, 2 ** 20, dtype=jnp.int32)
    column = jnp.arange(NB, dtype=jnp.int32)
    ranking = raw * NB + column[None, None, :]
    ranking = jnp.where(column[None, :, None] == column[None, None, :], 2 ** 30, ranking)
    chosen = jax.lax.top_k(ranking, KSEL)[1]
    return chosen.astype(jnp.int32)


def levels(key, shape, cuts, smallest, high):
    loudness = 1.0
    for dim, blocks in cuts:
        heights = jax.random.uniform(jax.random.fold_in(jax.random.fold_in(key, 6), dim), (blocks,), jnp.float32, smallest / len(cuts), high / len(cuts))
        loudness = loudness * jnp.repeat(jnp.exp(heights), shape[dim] // blocks).reshape((-1,) + (1,) * (len(shape) - 1 - dim))
    return loudness


def scatter_about(rng, shape, scale, reach, cuts=(), kind=jnp.bfloat16):
    values = scale * jax.random.normal(rng, shape, jnp.float32)
    if cuts:
        values = values * levels(rng, shape, cuts, -0.22, 0.18)
    return jnp.clip(values, -reach, reach).astype(kind)


def setup_inputs(seed: int = 0, part: int = 0) -> dict:
    key_of = jax.random.split(jax.random.key(seed), 6)
    part_keys = jax.random.split(jax.random.fold_in(key_of[5], part), 6)
    queries = draw_queries(jax.random.fold_in(jax.random.fold_in(key_of[5], part), 71), part)
    keys_in = draw_keys_in(jax.random.fold_in(jax.random.fold_in(key_of[5], part), 71), part)
    value_input = scatter_about(part_keys[2], (TOKENS, HEADS * HEAD_DIM), 1.0, 6.0, ((0, 16),))
    head_class = draw_head_class(jax.random.fold_in(jax.random.fold_in(key_of[5], part), 71), part)
    block_lists = draw_block_lists(jax.random.fold_in(jax.random.fold_in(key_of[5], part), 71), part)
    return {"queries": queries, "keys_in": keys_in, "value_input": value_input, "head_class": head_class, "block_lists": block_lists}


def head_attention(query_head_slice, key_head, value_head, dense_flag, head_lists):
    block_count = query_head_slice.shape[0] // BLOCK_LEN
    number_list = jnp.arange(block_count, dtype=jnp.int32)
    hits = jnp.any(head_lists[:, :, None] == number_list[None, None, :], axis=1)
    blocks = jnp.logical_or(hits, dense_flag == 1)
    allowed = jnp.repeat(jnp.repeat(blocks, BLOCK_LEN, axis=0), BLOCK_LEN, axis=1)
    scores = jnp.dot(query_head_slice, key_head.T, preferred_element_type=jnp.float32) * (1.0 / math.sqrt(HEAD_DIM))
    scores = jnp.where(allowed, scores, -jnp.inf)
    largest = lax.optimization_barrier(jnp.max(scores, axis=1, keepdims=True))
    weights = jnp.exp(scores - largest)
    total = lax.optimization_barrier(jnp.sum(weights, axis=1, keepdims=True))
    mixed = jnp.dot(weights.astype(jnp.bfloat16), value_head, preferred_element_type=jnp.float32) / total
    return mixed.astype(jnp.bfloat16)

def reference(queries, keys_in, value_input, head_class, block_lists):

    def divide_heads(matrix):
        return matrix.reshape(TOKENS, HEADS, HEAD_DIM).transpose(1, 0, 2)

    def one_head(items):
        return head_attention(items[0], items[1], items[2], items[3], items[4])
    outputs = lax.map(one_head, (divide_heads(queries), divide_heads(keys_in), divide_heads(value_input), head_class, block_lists))
    return outputs.transpose(1, 0, 2).reshape(TOKENS, HEADS * HEAD_DIM)
```

```python
import functools
import math

import jax
import jax.numpy as jnp
from jax import lax
from jax.experimental import pallas as pl
from jax.experimental.pallas import tpu as pltpu
from jax.sharding import PartitionSpec as P

MESH = pl.DeviceIdType.MESH
BLOCK_LEN = 128


def ring_delta(step, chips):
    return chips // 2 + (1 - 2 * (step % 2)) * ((step + 1) // 2)


def kernel(
    n, per, head_dim, q_ref, k_ref, v_ref, class_ref, lists_ref, out_ref,
    q_buf, k_buf, v_buf, o_buf, bias, class_mem, lists_mem,
    small_sem, send_sem, kv_sem, q_sem, o_send_sem, o_sem,
):
    me = lax.axis_index("seq")
    chips = n // 2
    chip, core = me // 2, me % 2
    rows = q_ref.shape[0]
    tokens = n * rows
    blocks = tokens // BLOCK_LEN

    class_copy = pltpu.make_async_copy(class_ref, class_mem, small_sem.at[0])
    class_copy.start()
    lists_copy = pltpu.make_async_copy(lists_ref, lists_mem, small_sem.at[1])
    lists_copy.start()

    def columns(device, head):
        return pl.ds(pl.multiple_of((device * per + head) * head_dim, head_dim), head_dim)

    def token_rows(device):
        return pl.ds(pl.multiple_of(device * rows, rows), rows)

    def tensors(head, target_row):
        return (
            (k_ref, k_buf, kv_sem.at[head, 0]),
            (v_ref, v_buf, kv_sem.at[head, 1]),
            (q_ref, q_buf, q_sem.at[head, target_row]),
        )

    barrier = pltpu.get_barrier_semaphore()

    def greet(d, carry):
        pl.semaphore_signal(
            barrier, inc=1, device_id={"seq": lax.rem(me + d, n)}, device_id_type=MESH
        )
        return carry

    lax.fori_loop(1, n, greet, 0)

    for head in range(per):
        for src, buf, sem in tensors(head, me):
            pltpu.make_async_copy(
                src.at[:, columns(me, head)], buf.at[head, token_rows(me)], sem
            ).start()

    pl.semaphore_wait(barrier, n - 1)

    def send_inputs(head, which):
        def to_peer(i, carry):
            step = i // 2
            target = lax.rem(chip + ring_delta(step, chips), chips) * 2 + (core + 1 - i % 2) % 2
            for t in which:
                src, buf, sem = tensors(head, me)[t]
                pltpu.make_async_remote_copy(
                    src_ref=src.at[:, columns(target, head)],
                    dst_ref=buf.at[head, token_rows(me)],
                    send_sem=send_sem.at[head, t],
                    recv_sem=sem,
                    device_id={"seq": target},
                    device_id_type=MESH,
                ).start()
            return carry

        lax.fori_loop(0, n - 1, to_peer, 0)

    for head in range(per):
        send_inputs(head, (0, 1))
        send_inputs(head, (2,))

    class_copy.wait()
    lists_copy.wait()
    key_block = lax.broadcasted_iota(jnp.int32, (blocks, tokens), 1) // BLOCK_LEN
    lists = lists_mem[...].astype(jnp.float32)
    head_lane = lax.broadcasted_iota(jnp.int32, (blocks, lists.shape[2]), 1)
    for head in range(per):
        mine = head_lane == me * per + head
        allowed = None
        for j in range(lists.shape[1]):
            listed = jnp.sum(jnp.where(mine, lists[:, j, :], 0.0), axis=1, keepdims=True)
            hit = listed.astype(jnp.int32) == key_block
            allowed = hit if allowed is None else jnp.logical_or(allowed, hit)
        closed = jnp.where(class_mem[me * per + head] == 1, 0.0, -jnp.inf)
        bias[head] = jnp.where(allowed, 0.0, closed)

    factor = math.log2(math.e) / math.sqrt(head_dim)

    for head in range(per):
        pltpu.make_async_copy(k_buf.at[head], k_buf.at[head], kv_sem.at[head, 0]).wait()
        pltpu.make_async_copy(v_buf.at[head], v_buf.at[head], kv_sem.at[head, 1]).wait()

        def attend(step, carry, head=head):
            source_chip = lax.rem(chip + 2 * chips - ring_delta(step, chips), chips)
            for half in range(2):
                device = source_chip * 2 + half
                pltpu.make_async_copy(
                    q_buf.at[head, token_rows(device)],
                    q_buf.at[head, token_rows(device)],
                    q_sem.at[head, device],
                ).wait()
            pair_rows = pl.ds(pl.multiple_of(source_chip * 2 * rows, 2 * rows), 2 * rows)
            scores = lax.dot_general(
                q_buf[head, pair_rows, :],
                k_buf[head],
                (((1,), (1,)), ((), ())),
                preferred_element_type=jnp.float32,
            )
            for half in range(2):
                device = source_chip * 2 + half
                part = scores[half * rows : (half + 1) * rows] + bias[head, pl.ds(device, 1), :]
                largest = jnp.max(part, axis=1, keepdims=True)
                weights = jnp.exp2((part - largest) * factor)
                total = jnp.sum(weights, axis=1, keepdims=True)
                mixed = lax.dot_general(
                    weights.astype(jnp.bfloat16),
                    v_buf[head],
                    (((1,), (0,)), ((), ())),
                    preferred_element_type=jnp.float32,
                )
                o_buf[head, token_rows(device), :] = (mixed / total).astype(jnp.bfloat16)

                @pl.when(device != me)
                def _():
                    pltpu.make_async_remote_copy(
                        src_ref=o_buf.at[head, token_rows(device)],
                        dst_ref=out_ref.at[:, columns(me, head)],
                        send_sem=o_send_sem,
                        recv_sem=o_sem,
                        device_id={"seq": device},
                        device_id_type=MESH,
                    ).start()

                @pl.when(device == me)
                def _():
                    pltpu.make_async_copy(
                        o_buf.at[head, token_rows(device)],
                        out_ref.at[:, columns(me, head)],
                        o_sem,
                    ).start()

            return carry

        lax.fori_loop(0, chips, attend, 0)

    sent = pl.ds(0, (n - 1) * rows)
    for head in range(per):
        for t in range(3):
            pltpu.make_async_copy(
                k_buf.at[head, sent], k_buf.at[head, sent], send_sem.at[head, t]
            ).wait()
    all_sent = o_buf.at[:, sent]
    pltpu.make_async_copy(all_sent, all_sent, o_send_sem).wait()
    pltpu.make_async_copy(out_ref, out_ref, o_sem).wait()


def local(queries, keys_in, value_input, head_class, block_lists):
    n = lax.axis_size("seq")
    rows, width = queries.shape
    heads = head_class.shape[0]
    per = heads // n
    head_dim = width // heads
    tokens = n * rows
    blocks = tokens // BLOCK_LEN
    hbm = pl.BlockSpec(memory_space=pltpu.HBM)
    buffer = pltpu.VMEM((per, tokens, head_dim), jnp.bfloat16)
    return pl.pallas_call(
        functools.partial(kernel, n, per, head_dim),
        out_shape=jax.ShapeDtypeStruct((rows, width), jnp.bfloat16),
        in_specs=[hbm] * 5,
        out_specs=hbm,
        scratch_shapes=[
            buffer,
            buffer,
            buffer,
            buffer,
            pltpu.VMEM((per, blocks, tokens), jnp.float32),
            pltpu.SMEM((heads,), jnp.int32),
            pltpu.VMEM(block_lists.shape[1:] + (heads,), jnp.int32),
            pltpu.SemaphoreType.DMA((2,)),
            pltpu.SemaphoreType.DMA((per, 3)),
            pltpu.SemaphoreType.DMA((per, 2)),
            pltpu.SemaphoreType.DMA((per, n)),
            pltpu.SemaphoreType.DMA,
            pltpu.SemaphoreType.DMA,
        ],
        compiler_params=pltpu.CompilerParams(
            collective_id=0, has_side_effects=True, vmem_limit_bytes=63 << 20
        ),
        cost_estimate=pl.CostEstimate(
            flops=4 * per * tokens * tokens * head_dim,
            bytes_accessed=8 * rows * width,
            transcendentals=per * tokens * tokens,
        ),
    )(queries, keys_in, value_input, head_class, jnp.transpose(block_lists, (1, 2, 0)))


def solution(mesh):
    placed = (
        P(("clip", "seq"), None),
        P(("clip", "seq"), None),
        P(("clip", "seq"), None),
        P("clip"),
        P("clip", None, None),
    )
    return jax.shard_map(
        local, mesh=mesh, in_specs=placed, out_specs=P(("clip", "seq"), None), check_vma=False
    )
```

```python
import functools
import math

import jax
import jax.numpy as jnp
from jax import lax
from jax.experimental import pallas as pl
from jax.experimental.pallas import tpu as pltpu
from jax.sharding import PartitionSpec as P

MESH = pl.DeviceIdType.MESH
BLOCK_LEN = 128


def ring_delta(step, chips):
    return (1 - 2 * (step % 2)) * ((step + 1) // 2) + (step==chips-1)*0


def kernel(
    n, per, head_dim, q_ref, k_ref, v_ref, class_ref, lists_ref, out_ref,
    q_buf, k_buf, v_buf, o_buf, bias, class_mem, lists_mem,
    small_sem, send_sem, kv_sem, q_sem, o_send_sem, o_sem,
):
    me = lax.axis_index("seq")
    chips = n // 2
    chip, core = me // 2, me % 2
    rows = q_ref.shape[0]
    tokens = n * rows
    blocks = tokens // BLOCK_LEN

    class_copy = pltpu.make_async_copy(class_ref, class_mem, small_sem.at[0])
    class_copy.start()
    lists_copy = pltpu.make_async_copy(lists_ref, lists_mem, small_sem.at[1])
    lists_copy.start()

    def columns(device, head):
        return pl.ds(pl.multiple_of((device * per + head) * head_dim, head_dim), head_dim)

    def token_rows(device):
        return pl.ds(pl.multiple_of(device * rows, rows), rows)

    def tensors(head, target_row):
        return (
            (k_ref, k_buf, kv_sem.at[head, 0]),
            (v_ref, v_buf, kv_sem.at[head, 1]),
            (q_ref, q_buf, q_sem.at[head, target_row]),
        )

    barrier = pltpu.get_barrier_semaphore()

    def greet(d, carry):
        pl.semaphore_signal(
            barrier, inc=1, device_id={"seq": lax.rem(me + d, n)}, device_id_type=MESH
        )
        return carry

    lax.fori_loop(1, n, greet, 0)

    for head in range(per):
        for src, buf, sem in tensors(head, me):
            pltpu.make_async_copy(
                src.at[:, columns(me, head)], buf.at[head, token_rows(me)], sem
            ).start()

    pl.semaphore_wait(barrier, n - 1)

    def send_inputs(head, which):
        def to_peer(i, carry):
            step = i // 2
            target = lax.rem(chip + chips + ring_delta((i+1)//2, chips), chips) * 2 + (core + (i+1) % 2) % 2
            for t in which:
                src, buf, sem = tensors(head, me)[t]
                pltpu.make_async_remote_copy(
                    src_ref=src.at[:, columns(target, head)],
                    dst_ref=buf.at[head, token_rows(me)],
                    send_sem=send_sem.at[head, t],
                    recv_sem=sem,
                    device_id={"seq": target},
                    device_id_type=MESH,
                ).start()
            return carry

        lax.fori_loop(0, n - 1, to_peer, 0)

    for head in range(per):
        send_inputs(head, (0, 1))
        send_inputs(head, (2,))

    class_copy.wait()
    lists_copy.wait()
    key_block = lax.broadcasted_iota(jnp.int32, (blocks, tokens), 1) // BLOCK_LEN
    lists = lists_mem[...].astype(jnp.float32)
    head_lane = lax.broadcasted_iota(jnp.int32, (blocks, lists.shape[2]), 1)
    for head in range(per):
        mine = head_lane == me * per + head
        allowed = None
        for j in range(lists.shape[1]):
            listed = jnp.sum(jnp.where(mine, lists[:, j, :], 0.0), axis=1, keepdims=True)
            hit = listed.astype(jnp.int32) == key_block
            allowed = hit if allowed is None else jnp.logical_or(allowed, hit)
        closed = jnp.where(class_mem[me * per + head] == 1, 0.0, -jnp.inf)
        bias[head] = jnp.where(allowed, 0.0, closed)

    factor = math.log2(math.e) / math.sqrt(head_dim)

    for head in range(per):
        pltpu.make_async_copy(k_buf.at[head], k_buf.at[head], kv_sem.at[head, 0]).wait()
        pltpu.make_async_copy(v_buf.at[head], v_buf.at[head], kv_sem.at[head, 1]).wait()

        def attend(step, carry, head=head):
            source_chip = lax.rem(chip + 2 * chips - ring_delta(step, chips), chips)
            for half in range(2):
                device = source_chip * 2 + half
                pltpu.make_async_copy(
                    q_buf.at[head, token_rows(device)],
                    q_buf.at[head, token_rows(device)],
                    q_sem.at[head, device],
                ).wait()
            pair_rows = pl.ds(pl.multiple_of(source_chip * 2 * rows, 2 * rows), 2 * rows)
            scores = lax.dot_general(
                q_buf[head, pair_rows, :],
                k_buf[head],
                (((1,), (1,)), ((), ())),
                preferred_element_type=jnp.float32,
            )
            for half in range(2):
                device = source_chip * 2 + half
                part = scores[half * rows : (half + 1) * rows] + bias[head, pl.ds(device, 1), :]
                largest = jnp.max(part, axis=1, keepdims=True)
                weights = jnp.exp2((part - largest) * factor)
                total = jnp.sum(weights, axis=1, keepdims=True)
                mixed = lax.dot_general(
                    weights.astype(jnp.bfloat16),
                    v_buf[head],
                    (((1,), (0,)), ((), ())),
                    preferred_element_type=jnp.float32,
                )
                o_buf[head, token_rows(device), :] = (mixed / total).astype(jnp.bfloat16)

                @pl.when(device != me)
                def _():
                    pltpu.make_async_remote_copy(
                        src_ref=o_buf.at[head, token_rows(device)],
                        dst_ref=out_ref.at[:, columns(me, head)],
                        send_sem=o_send_sem,
                        recv_sem=o_sem,
                        device_id={"seq": device},
                        device_id_type=MESH,
                    ).start()

                @pl.when(device == me)
                def _():
                    pltpu.make_async_copy(
                        o_buf.at[head, token_rows(device)],
                        out_ref.at[:, columns(me, head)],
                        o_sem,
                    ).start()

            return carry

        lax.fori_loop(0, chips, attend, 0)

    sent = pl.ds(0, (n - 1) * rows)
    for head in range(per):
        for t in range(3):
            pltpu.make_async_copy(
                k_buf.at[head, sent], k_buf.at[head, sent], send_sem.at[head, t]
            ).wait()
    all_sent = o_buf.at[:, sent]
    pltpu.make_async_copy(all_sent, all_sent, o_send_sem).wait()
    pltpu.make_async_copy(out_ref, out_ref, o_sem).wait()


def local(queries, keys_in, value_input, head_class, block_lists):
    n = lax.axis_size("seq")
    rows, width = queries.shape
    heads = head_class.shape[0]
    per = heads // n
    head_dim = width // heads
    tokens = n * rows
    blocks = tokens // BLOCK_LEN
    hbm = pl.BlockSpec(memory_space=pltpu.HBM)
    buffer = pltpu.VMEM((per, tokens, head_dim), jnp.bfloat16)
    return pl.pallas_call(
        functools.partial(kernel, n, per, head_dim),
        out_shape=pltpu.VMEM((rows, width), jnp.bfloat16),
        in_specs=[hbm] * 5,
        out_specs=pl.BlockSpec(memory_space=pltpu.VMEM),
        scratch_shapes=[
            buffer,
            buffer,
            buffer,
            buffer,
            pltpu.VMEM((per, blocks, tokens), jnp.float32),
            pltpu.SMEM((heads,), jnp.int32),
            pltpu.VMEM(block_lists.shape[1:] + (heads,), jnp.int32),
            pltpu.SemaphoreType.DMA((2,)),
            pltpu.SemaphoreType.DMA((per, 3)),
            pltpu.SemaphoreType.DMA((per, 2)),
            pltpu.SemaphoreType.DMA((per, n)),
            pltpu.SemaphoreType.DMA,
            pltpu.SemaphoreType.DMA,
        ],
        compiler_params=pltpu.CompilerParams(
            collective_id=0, has_side_effects=True, vmem_limit_bytes=48 << 20
        ),
        cost_estimate=pl.CostEstimate(
            flops=4 * per * tokens * tokens * head_dim,
            bytes_accessed=8 * rows * width,
            transcendentals=per * tokens * tokens,
        ),
    )(
        *(
            pltpu.with_memory_space_constraint(x, pltpu.HBM)
            for x in (queries, keys_in, value_input, head_class, jnp.transpose(block_lists, (1, 2, 0)))
        )
    )


def solution(mesh):
    placed = (
        P(("clip", "seq"), None),
        P(("clip", "seq"), None),
        P(("clip", "seq"), None),
        P("clip"),
        P("clip", None, None),
    )
    return jax.shard_map(
        local, mesh=mesh, in_specs=placed, out_specs=P(("clip", "seq"), None), check_vma=False
    )
```

```python
import functools
import math

import jax
import jax.numpy as jnp
from jax import lax
from jax.experimental import pallas as pl
from jax.experimental.pallas import tpu as pltpu
from jax.sharding import PartitionSpec as P

MESH = pl.DeviceIdType.MESH
BLOCK_LEN = 128


def ring_delta(step):
    return (2 * (step % 2) - 1) * ((step + 1) // 2)


def kernel(
    n, per, head_dim, q_ref, k_ref, v_ref, class_ref, lists_ref, out_ref,
    q_buf, k_buf, v_buf, o_buf, bias, class_mem, lists_mem,
    late_sem, small_sem, send_sem, kv_sem, q_sem, o_send_sem, o_sem,
):
    me = lax.axis_index("seq")
    chips = n // 2
    chip, core = me // 2, me % 2
    rows = q_ref.shape[0]
    tokens = n * rows
    blocks = tokens // BLOCK_LEN

    class_copy = pltpu.make_async_copy(class_ref, class_mem, small_sem.at[0])
    class_copy.start()
    lists_copy = pltpu.make_async_copy(lists_ref, lists_mem, small_sem.at[1])
    lists_copy.start()

    def columns(device, head):
        return pl.ds(pl.multiple_of((device * per + head) * head_dim, head_dim), head_dim)

    def token_rows(device):
        return pl.ds(pl.multiple_of(device * rows, rows), rows)

    def tensors(head, target_row):
        return (
            (k_ref, k_buf, kv_sem.at[head, 0]),
            (v_ref, v_buf, kv_sem.at[head, 1]),
            (q_ref, q_buf, q_sem.at[head, target_row]),
        )

    barrier = pltpu.get_barrier_semaphore()
    has_late = lax.axis_index("clip") == 0
    is_late = jnp.logical_and(has_late, me == 0)

    def others(d):
        return lax.rem(me + d, n)

    def greet(d, carry):
        pl.semaphore_signal(
            barrier, inc=1, device_id={"seq": others(d)}, device_id_type=MESH
        )
        return carry

    @pl.when(jnp.logical_not(is_late))
    def _():
        lax.fori_loop(1, n, greet, 0)

    for head in range(per):
        for src, buf, sem in tensors(head, me):
            pltpu.make_async_copy(
                src.at[:, columns(me, head)], buf.at[head, token_rows(me)], sem
            ).start()

    pl.semaphore_wait(
        barrier, jnp.where(jnp.logical_and(has_late, me > 0), n - 2, n - 1)
    )

    def answer(d, carry):
        pl.semaphore_signal(
            late_sem, inc=1, device_id={"seq": others(d)}, device_id_type=MESH
        )
        return carry

    @pl.when(is_late)
    def _():
        lax.fori_loop(1, n, answer, 0)

    def peer(i):
        target_chip = lax.rem(chip + chips + ring_delta((i + 1) // 2), chips)
        return target_chip * 2 + (core + (i + 1) % 2) % 2

    def send(target, head):
        for t, (src, buf, sem) in enumerate(tensors(head, me)):
            pltpu.make_async_remote_copy(
                src_ref=src.at[:, columns(target, head)],
                dst_ref=buf.at[head, token_rows(me)],
                send_sem=send_sem.at[head, t],
                recv_sem=sem,
                device_id={"seq": target},
                device_id_type=MESH,
            ).start()

    def first_head(i, carry):
        target = peer(i)

        @pl.when(jnp.logical_not(jnp.logical_and(has_late, target == 0)))
        def _():
            send(target, 0)

        return carry

    lax.fori_loop(0, n - 1, first_head, 0)

    @pl.when(jnp.logical_and(has_late, me > 0))
    def _():
        pl.semaphore_wait(late_sem, 1)
        send(0, 0)

    def later_head(i, carry, head):
        send(peer(i), head)
        return carry

    for head in range(1, per):
        lax.fori_loop(0, n - 1, functools.partial(later_head, head=head), 0)

    class_copy.wait()
    lists_copy.wait()
    key_block = lax.broadcasted_iota(jnp.int32, (blocks, tokens), 1) // BLOCK_LEN
    lists = lists_mem[...].astype(jnp.float32)
    head_lane = lax.broadcasted_iota(jnp.int32, (blocks, lists.shape[2]), 1)
    for head in range(per):
        mine = head_lane == me * per + head
        allowed = None
        for j in range(lists.shape[1]):
            listed = jnp.sum(jnp.where(mine, lists[:, j, :], 0.0), axis=1, keepdims=True)
            hit = listed.astype(jnp.int32) == key_block
            allowed = hit if allowed is None else jnp.logical_or(allowed, hit)
        closed = jnp.where(class_mem[me * per + head] == 1, 0.0, -jnp.inf)
        bias[head] = jnp.where(allowed, 0.0, closed)

    factor = math.log2(math.e) / math.sqrt(head_dim)

    for head in range(per):
        pltpu.make_async_copy(k_buf.at[head], k_buf.at[head], kv_sem.at[head, 0]).wait()
        pltpu.make_async_copy(v_buf.at[head], v_buf.at[head], kv_sem.at[head, 1]).wait()

        def attend(step, carry, head=head):
            source_chip = lax.rem(chip + chips - ring_delta(step), chips)
            for half in range(2):
                device = source_chip * 2 + half
                pltpu.make_async_copy(
                    q_buf.at[head, token_rows(device)],
                    q_buf.at[head, token_rows(device)],
                    q_sem.at[head, device],
                ).wait()
            pair_rows = pl.ds(pl.multiple_of(source_chip * 2 * rows, 2 * rows), 2 * rows)
            scores = lax.dot_general(
                q_buf[head, pair_rows, :],
                k_buf[head],
                (((1,), (1,)), ((), ())),
                preferred_element_type=jnp.float32,
            )
            for half in range(2):
                device = source_chip * 2 + half
                part = scores[half * rows : (half + 1) * rows] + bias[head, pl.ds(device, 1), :]
                largest = jnp.max(part, axis=1, keepdims=True)
                weights = jnp.exp2((part - largest) * factor)
                total = jnp.sum(weights, axis=1, keepdims=True)
                mixed = lax.dot_general(
                    weights.astype(jnp.bfloat16),
                    v_buf[head],
                    (((1,), (0,)), ((), ())),
                    preferred_element_type=jnp.float32,
                )
                o_buf[head, token_rows(device), :] = (mixed / total).astype(jnp.bfloat16)

                @pl.when(device != me)
                def _():
                    pltpu.make_async_remote_copy(
                        src_ref=o_buf.at[head, token_rows(device)],
                        dst_ref=out_ref.at[:, columns(me, head)],
                        send_sem=o_send_sem,
                        recv_sem=o_sem,
                        device_id={"seq": device},
                        device_id_type=MESH,
                    ).start()

                @pl.when(device == me)
                def _():
                    pltpu.make_async_copy(
                        o_buf.at[head, token_rows(device)],
                        out_ref.at[:, columns(me, head)],
                        o_sem,
                    ).start()

            return carry

        lax.fori_loop(0, chips, attend, 0)

    sent = pl.ds(0, (n - 1) * rows)
    for head in range(per):
        for t in range(3):
            pltpu.make_async_copy(
                k_buf.at[head, sent], k_buf.at[head, sent], send_sem.at[head, t]
            ).wait()
    all_sent = o_buf.at[:, sent]
    pltpu.make_async_copy(all_sent, all_sent, o_send_sem).wait()
    pltpu.make_async_copy(out_ref, out_ref, o_sem).wait()


def local(queries, keys_in, value_input, head_class, block_lists):
    n = lax.axis_size("seq")
    rows, width = queries.shape
    heads = head_class.shape[0]
    per = heads // n
    head_dim = width // heads
    tokens = n * rows
    blocks = tokens // BLOCK_LEN
    hbm = pl.BlockSpec(memory_space=pltpu.HBM)
    buffer = pltpu.VMEM((per, tokens, head_dim), jnp.bfloat16)
    return pl.pallas_call(
        functools.partial(kernel, n, per, head_dim),
        out_shape=pltpu.VMEM((rows, width), jnp.bfloat16),
        in_specs=[hbm] * 5,
        out_specs=pl.BlockSpec(memory_space=pltpu.VMEM),
        scratch_shapes=[
            buffer,
            buffer,
            buffer,
            buffer,
            pltpu.VMEM((per, blocks, tokens), jnp.float32),
            pltpu.SMEM((heads,), jnp.int32),
            pltpu.VMEM(block_lists.shape[1:] + (heads,), jnp.int32),
            pltpu.SemaphoreType.REGULAR,
            pltpu.SemaphoreType.DMA((2,)),
            pltpu.SemaphoreType.DMA((per, 3)),
            pltpu.SemaphoreType.DMA((per, 2)),
            pltpu.SemaphoreType.DMA((per, n)),
            pltpu.SemaphoreType.DMA,
            pltpu.SemaphoreType.DMA,
        ],
        compiler_params=pltpu.CompilerParams(
            collective_id=0, has_side_effects=True, vmem_limit_bytes=48 << 20
        ),
        cost_estimate=pl.CostEstimate(
            flops=4 * per * tokens * tokens * head_dim,
            bytes_accessed=8 * rows * width,
            transcendentals=per * tokens * tokens,
        ),
    )(
        *(
            pltpu.with_memory_space_constraint(x, pltpu.HBM)
            for x in (queries, keys_in, value_input, head_class, jnp.transpose(block_lists, (1, 2, 0)))
        )
    )


def solution(mesh):
    placed = (
        P(("clip", "seq"), None),
        P(("clip", "seq"), None),
        P(("clip", "seq"), None),
        P("clip"),
        P("clip", None, None),
    )
    return jax.shard_map(
        local, mesh=mesh, in_specs=placed, out_specs=P(("clip", "seq"), None), check_vma=False
    )
```

```python
import functools
import math

import jax
import jax.numpy as jnp
from jax import lax
from jax.experimental import pallas as pl
from jax.experimental.pallas import tpu as pltpu
from jax.sharding import PartitionSpec as P

MESH = pl.DeviceIdType.MESH
BLOCK_LEN = 128


def ring_delta(step):
    return (2 * (step % 2) - 1) * ((step + 1) // 2)


def early_first(chip, step, early, chips):
    out = step
    seen = early
    for k in range(chips):
        other = lax.rem(chip + 2 * chips - ring_delta(chips - 1 - k), chips)
        is_new = other >= early
        out = jnp.where(jnp.logical_and(is_new, step == seen), other, out)
        seen = seen + is_new.astype(jnp.int32)
    return out


def kernel(
    n, per, head_dim, q_ref, k_ref, v_ref, class_ref, lists_ref, out_ref,
    q_buf, k_buf, v_buf, o_buf, bias, class_mem, lists_mem,
    late_sem, wave_sem, small_sem, send_sem, kv_sem, q_sem, o_send_sem, o_sem,
):
    me = lax.axis_index("seq")
    chips = n // 2
    chip, core = me // 2, me % 2
    rows = q_ref.shape[0]
    tokens = n * rows
    blocks = tokens // BLOCK_LEN

    def columns(device, head):
        return pl.ds(pl.multiple_of((device * per + head) * head_dim, head_dim), head_dim)

    def token_rows(device):
        return pl.ds(pl.multiple_of(device * rows, rows), rows)

    def tensors(head, target_row):
        return (
            (k_ref, k_buf, kv_sem.at[head, 0]),
            (v_ref, v_buf, kv_sem.at[head, 1]),
            (q_ref, q_buf, q_sem.at[head, target_row]),
        )

    barrier = pltpu.get_barrier_semaphore()
    has_late = lax.axis_index("clip") == 0
    is_late = jnp.logical_and(has_late, me == 0)
    on_time = jnp.logical_not(is_late)

    def at(distance, which):
        return lax.rem(chip + chips + distance, chips) * 2 + which

    def signal(sem, target):
        pl.semaphore_signal(sem, inc=1, device_id={"seq": target}, device_id_type=MESH)

    near = (at(0, 1 - core), at(1, 0), at(1, 1), at(-1, 0), at(-1, 1))

    @pl.when(on_time)
    def _():
        for target in near:
            signal(barrier, target)

    @pl.when(jnp.logical_and(has_late, jnp.logical_and(chip > 1, chip < chips - 1)))
    def _():
        signal(barrier, 0)

    class_copy = pltpu.make_async_copy(class_ref, class_mem, small_sem.at[0])
    class_copy.start()
    lists_copy = pltpu.make_async_copy(lists_ref, lists_mem, small_sem.at[1])
    lists_copy.start()

    for head in range(per):
        for src, buf, sem in tensors(head, me):
            pltpu.make_async_copy(
                src.at[:, columns(me, head)], buf.at[head, token_rows(me)], sem
            ).start()

    beside_late = jnp.logical_and(has_late, jnp.logical_or(chip <= 1, chip == chips - 1))
    few = jnp.where(beside_late, len(near) - 1, len(near))
    pl.semaphore_wait(barrier, jnp.where(is_late, n - 1, few))

    def answer(d, carry):
        signal(late_sem, lax.rem(me + d, n))
        return carry

    @pl.when(is_late)
    def _():
        lax.fori_loop(1, n, answer, 0)

    def unless_late(target, act):
        pl.when(jnp.logical_not(jnp.logical_and(has_late, target == 0)))(act)

    def tell(side, wave):
        for which in range(2):
            target = at(side, which)
            unless_late(target, lambda: signal(wave_sem.at[(1 - side) // 2, wave - 2], target))

    def hear(side, wave):
        told = jnp.where(jnp.logical_and(has_late, at(side, 0) == 0), 1, 2)
        pl.semaphore_wait(wave_sem.at[(1 + side) // 2, wave - 2], told)

    def send(target, head):
        for t, (src, buf, sem) in enumerate(tensors(head, me)):
            pltpu.make_async_remote_copy(
                src_ref=src.at[:, columns(target, head)],
                dst_ref=buf.at[head, token_rows(me)],
                send_sem=send_sem.at[head, t],
                recv_sem=sem,
                device_id={"seq": target},
                device_id_type=MESH,
            ).start()

    def send_first(distance):
        def one(which, carry):
            target = at(distance, which)
            unless_late(target, lambda: send(target, 0))
            return carry

        lax.fori_loop(0, 2, one, 0)

    @pl.when(on_time)
    def _():
        tell(-1, 2)
        tell(1, 2)

    unless_late(near[0], lambda: send(near[0], 0))
    send_first(1)
    send_first(-1)
    for wave in range(2, chips // 2 + 1):

        @pl.when(on_time)
        def _():
            hear(1, wave)
            if wave < chips // 2:
                tell(-1, wave + 1)
                hear(-1, wave)
            if wave + 1 < chips // 2:
                tell(1, wave + 1)

        send_first(wave)
        if wave < chips // 2:
            send_first(-wave)

    @pl.when(jnp.logical_and(has_late, me > 0))
    def _():
        pl.semaphore_wait(late_sem, 1)
        send(0, 0)

    def peer(i):
        target_chip = lax.rem(chip + chips + ring_delta((i + 1) // 2), chips)
        return target_chip * 2 + (core + (i + 1) % 2) % 2

    def later_head(i, carry, head):
        send(peer(i), head)
        return carry

    for head in range(1, per):
        lax.fori_loop(0, n - 1, functools.partial(later_head, head=head), 0)

    class_copy.wait()
    lists_copy.wait()
    key_block = lax.broadcasted_iota(jnp.int32, (blocks, tokens), 1) // BLOCK_LEN
    lists = lists_mem[...].astype(jnp.float32)
    head_lane = lax.broadcasted_iota(jnp.int32, (blocks, lists.shape[2]), 1)
    for head in range(per):
        mine = head_lane == me * per + head
        allowed = None
        for j in range(lists.shape[1]):
            listed = jnp.sum(jnp.where(mine, lists[:, j, :], 0.0), axis=1, keepdims=True)
            hit = listed.astype(jnp.int32) == key_block
            allowed = hit if allowed is None else jnp.logical_or(allowed, hit)
        closed = jnp.where(class_mem[me * per + head] == 1, 0.0, -jnp.inf)
        bias[head] = jnp.where(allowed, 0.0, closed)

    factor = math.log2(math.e) / math.sqrt(head_dim)

    for head in range(per):
        pltpu.make_async_copy(k_buf.at[head], k_buf.at[head], kv_sem.at[head, 0]).wait()
        pltpu.make_async_copy(v_buf.at[head], v_buf.at[head], kv_sem.at[head, 1]).wait()

        def attend(step, carry, head=head):
            source_chip = early_first(chip, step, 2, chips)
            for half in range(2):
                device = source_chip * 2 + half
                pltpu.make_async_copy(
                    q_buf.at[head, token_rows(device)],
                    q_buf.at[head, token_rows(device)],
                    q_sem.at[head, device],
                ).wait()
            pair_rows = pl.ds(pl.multiple_of(source_chip * 2 * rows, 2 * rows), 2 * rows)
            scores = lax.dot_general(
                q_buf[head, pair_rows, :],
                k_buf[head],
                (((1,), (1,)), ((), ())),
                preferred_element_type=jnp.float32,
            )
            for half in range(2):
                device = source_chip * 2 + half
                part = scores[half * rows : (half + 1) * rows] + bias[head, pl.ds(device, 1), :]
                largest = jnp.max(part, axis=1, keepdims=True)
                weights = jnp.exp2((part - largest) * factor)
                total = jnp.sum(weights, axis=1, keepdims=True)
                mixed = lax.dot_general(
                    weights.astype(jnp.bfloat16),
                    v_buf[head],
                    (((1,), (0,)), ((), ())),
                    preferred_element_type=jnp.float32,
                )
                o_buf[head, token_rows(device), :] = (mixed / total).astype(jnp.bfloat16)

                @pl.when(device != me)
                def _():
                    pltpu.make_async_remote_copy(
                        src_ref=o_buf.at[head, token_rows(device)],
                        dst_ref=out_ref.at[:, columns(me, head)],
                        send_sem=o_send_sem,
                        recv_sem=o_sem,
                        device_id={"seq": device},
                        device_id_type=MESH,
                    ).start()

                @pl.when(device == me)
                def _():
                    pltpu.make_async_copy(
                        o_buf.at[head, token_rows(device)],
                        out_ref.at[:, columns(me, head)],
                        o_sem,
                    ).start()

            return carry

        lax.fori_loop(0, chips, attend, 0)

    sent = pl.ds(0, (n - 1) * rows)
    for head in range(per):
        for t in range(3):
            pltpu.make_async_copy(
                k_buf.at[head, sent], k_buf.at[head, sent], send_sem.at[head, t]
            ).wait()
    all_sent = o_buf.at[:, sent]
    pltpu.make_async_copy(all_sent, all_sent, o_send_sem).wait()
    pltpu.make_async_copy(out_ref, out_ref, o_sem).wait()


def local(queries, keys_in, value_input, head_class, block_lists):
    n = lax.axis_size("seq")
    rows, width = queries.shape
    heads = head_class.shape[0]
    per = heads // n
    head_dim = width // heads
    tokens = n * rows
    blocks = tokens // BLOCK_LEN
    hbm = pl.BlockSpec(memory_space=pltpu.HBM)
    buffer = pltpu.VMEM((per, tokens, head_dim), jnp.bfloat16)
    return pl.pallas_call(
        functools.partial(kernel, n, per, head_dim),
        out_shape=pltpu.VMEM((rows, width), jnp.bfloat16),
        in_specs=[hbm] * 5,
        out_specs=pl.BlockSpec(memory_space=pltpu.VMEM),
        scratch_shapes=[
            buffer,
            buffer,
            buffer,
            buffer,
            pltpu.VMEM((per, blocks, tokens), jnp.float32),
            pltpu.SMEM((heads,), jnp.int32),
            pltpu.VMEM(block_lists.shape[1:] + (heads,), jnp.int32),
            pltpu.SemaphoreType.REGULAR,
            pltpu.SemaphoreType.REGULAR((2, n // 4 - 1)),
            pltpu.SemaphoreType.DMA((2,)),
            pltpu.SemaphoreType.DMA((per, 3)),
            pltpu.SemaphoreType.DMA((per, 2)),
            pltpu.SemaphoreType.DMA((per, n)),
            pltpu.SemaphoreType.DMA,
            pltpu.SemaphoreType.DMA,
        ],
        compiler_params=pltpu.CompilerParams(
            collective_id=0, has_side_effects=True, vmem_limit_bytes=48 << 20
        ),
        cost_estimate=pl.CostEstimate(
            flops=4 * per * tokens * tokens * head_dim,
            bytes_accessed=8 * rows * width,
            transcendentals=per * tokens * tokens,
        ),
    )(
        *(
            pltpu.with_memory_space_constraint(x, pltpu.HBM)
            for x in (queries, keys_in, value_input, head_class, jnp.transpose(block_lists, (1, 2, 0)))
        )
    )


def solution(mesh):
    placed = (
        P(("clip", "seq"), None),
        P(("clip", "seq"), None),
        P(("clip", "seq"), None),
        P("clip"),
        P("clip", None, None),
    )
    return jax.shard_map(
        local, mesh=mesh, in_specs=placed, out_specs=P(("clip", "seq"), None), check_vma=False
    )
```

```python
import functools
import math

import jax
import jax.numpy as jnp
from jax import lax
from jax.experimental import pallas as pl
from jax.experimental.pallas import tpu as pltpu
from jax.sharding import PartitionSpec as P

MESH = pl.DeviceIdType.MESH
BLOCK_LEN = 128
EARLY = (0,)


def ring_delta(step):
    return (2 * (step % 2) - 1) * ((step + 1) // 2)


def service(chip, step, chips):
    out = EARLY[0]
    for k in range(1, len(EARLY)):
        out = jnp.where(step == k, EARLY[k], out)
    seen = len(EARLY)
    for k in range(chips):
        other = lax.rem(chip + 2 * chips - ring_delta(chips - 1 - k), chips)
        fresh = other >= 0
        for e in EARLY:
            fresh = jnp.logical_and(fresh, other != e)
        out = jnp.where(jnp.logical_and(fresh, step == seen), other, out)
        seen = seen + fresh.astype(jnp.int32)
    return out


def kernel(
    n, per, head_dim, q_ref, k_ref, v_ref, class_ref, lists_ref, out_ref,
    q_buf, k_buf, v_buf, o_buf, bias, class_mem, lists_mem,
    late_sem, wave_sem, small_sem, send_sem, kv_sem, q_sem, o_send_sem, o_sem,
):
    me = lax.axis_index("seq")
    chips = n // 2
    chip, core = me // 2, me % 2
    rows = q_ref.shape[0]
    tokens = n * rows
    blocks = tokens // BLOCK_LEN

    def columns(device, head):
        return pl.ds(pl.multiple_of((device * per + head) * head_dim, head_dim), head_dim)

    def token_rows(device):
        return pl.ds(pl.multiple_of(device * rows, rows), rows)

    def tensors(head, target_row):
        return (
            (k_ref, k_buf, kv_sem.at[head, 0]),
            (v_ref, v_buf, kv_sem.at[head, 1]),
            (q_ref, q_buf, q_sem.at[head, target_row]),
        )

    barrier = pltpu.get_barrier_semaphore()
    has_late = lax.axis_index("clip") == 0
    is_late = jnp.logical_and(has_late, me == 0)
    on_time = jnp.logical_not(is_late)

    def at(distance, which):
        return lax.rem(chip + chips + distance, chips) * 2 + which

    def signal(sem, target):
        pl.semaphore_signal(sem, inc=1, device_id={"seq": target}, device_id_type=MESH)

    near = (at(0, 1 - core), at(1, 0), at(1, 1), at(-1, 0), at(-1, 1))

    @pl.when(on_time)
    def _():
        for target in near:
            signal(barrier, target)

    @pl.when(jnp.logical_and(has_late, jnp.logical_and(chip > 1, chip < chips - 1)))
    def _():
        signal(barrier, 0)

    class_copy = pltpu.make_async_copy(class_ref, class_mem, small_sem.at[0])
    class_copy.start()
    lists_copy = pltpu.make_async_copy(lists_ref, lists_mem, small_sem.at[1])
    lists_copy.start()

    for head in range(per):
        for src, buf, sem in tensors(head, me):
            pltpu.make_async_copy(
                src.at[:, columns(me, head)], buf.at[head, token_rows(me)], sem
            ).start()

    beside_late = jnp.logical_and(has_late, jnp.logical_or(chip <= 1, chip == chips - 1))
    few = jnp.where(beside_late, len(near) - 1, len(near))
    pl.semaphore_wait(barrier, jnp.where(is_late, n - 1, few))

    def answer(d, carry):
        signal(late_sem, lax.rem(me + d, n))
        return carry

    @pl.when(is_late)
    def _():
        lax.fori_loop(1, n, answer, 0)

    def unless_late(target, act):
        pl.when(jnp.logical_not(jnp.logical_and(has_late, target == 0)))(act)

    def tell(side, wave):
        for which in range(2):
            target = at(side, which)
            unless_late(target, lambda: signal(wave_sem.at[(1 - side) // 2, wave - 2], target))

    def hear(side, wave):
        told = jnp.where(jnp.logical_and(has_late, at(side, 0) == 0), 1, 2)
        pl.semaphore_wait(wave_sem.at[(1 + side) // 2, wave - 2], told)

    def send(target, head):
        for t, (src, buf, sem) in enumerate(tensors(head, me)):
            pltpu.make_async_remote_copy(
                src_ref=src.at[:, columns(target, head)],
                dst_ref=buf.at[head, token_rows(me)],
                send_sem=send_sem.at[head, t],
                recv_sem=sem,
                device_id={"seq": target},
                device_id_type=MESH,
            ).start()

    def send_first(distance):
        def one(which, carry):
            target = at(distance, which)
            unless_late(target, lambda: send(target, 0))
            return carry

        lax.fori_loop(0, 2, one, 0)

    @pl.when(on_time)
    def _():
        tell(-1, 2)
        tell(1, 2)

    unless_late(near[0], lambda: send(near[0], 0))
    send_first(1)
    send_first(-1)
    for wave in range(2, chips // 2 + 1):

        @pl.when(on_time)
        def _():
            hear(1, wave)
            if wave < chips // 2:
                tell(-1, wave + 1)
                hear(-1, wave)
            if wave + 1 < chips // 2:
                tell(1, wave + 1)

        send_first(wave)
        if wave < chips // 2:
            send_first(-wave)

    @pl.when(jnp.logical_and(has_late, me > 0))
    def _():
        pl.semaphore_wait(late_sem, 1)
        send(0, 0)

    def peer(i):
        target_chip = lax.rem(chip + chips + ring_delta((i + 1) // 2), chips)
        return target_chip * 2 + (core + (i + 1) % 2) % 2

    def later_head(i, carry, head):
        send(peer(i), head)
        return carry

    for head in range(1, per):
        lax.fori_loop(0, n - 1, functools.partial(later_head, head=head), 0)

    class_copy.wait()
    lists_copy.wait()
    key_block = lax.broadcasted_iota(jnp.int32, (blocks, tokens), 1) // BLOCK_LEN
    lists = lists_mem[...].astype(jnp.float32)
    head_lane = lax.broadcasted_iota(jnp.int32, (blocks, lists.shape[2]), 1)
    for head in range(per):
        mine = head_lane == me * per + head
        allowed = None
        for j in range(lists.shape[1]):
            listed = jnp.sum(jnp.where(mine, lists[:, j, :], 0.0), axis=1, keepdims=True)
            hit = listed.astype(jnp.int32) == key_block
            allowed = hit if allowed is None else jnp.logical_or(allowed, hit)
        closed = jnp.where(class_mem[me * per + head] == 1, 0.0, -jnp.inf)
        bias[head] = jnp.where(allowed, 0.0, closed)

    factor = math.log2(math.e) / math.sqrt(head_dim)

    for head in range(per):
        pltpu.make_async_copy(k_buf.at[head], k_buf.at[head], kv_sem.at[head, 0]).wait()
        pltpu.make_async_copy(v_buf.at[head], v_buf.at[head], kv_sem.at[head, 1]).wait()

        def attend(step, carry, head=head):
            source_chip = service(chip, step, chips)
            for half in range(2):
                device = source_chip * 2 + half
                pltpu.make_async_copy(
                    q_buf.at[head, token_rows(device)],
                    q_buf.at[head, token_rows(device)],
                    q_sem.at[head, device],
                ).wait()
            pair_rows = pl.ds(pl.multiple_of(source_chip * 2 * rows, 2 * rows), 2 * rows)
            scores = lax.dot_general(
                q_buf[head, pair_rows, :],
                k_buf[head],
                (((1,), (1,)), ((), ())),
                preferred_element_type=jnp.float32,
            )
            for half in (1, 0):
                device = source_chip * 2 + half
                part = scores[half * rows : (half + 1) * rows] + bias[head, pl.ds(device, 1), :]
                largest = jnp.max(part, axis=1, keepdims=True)
                weights = jnp.exp2((part - largest) * factor)
                total = jnp.sum(weights, axis=1, keepdims=True)
                mixed = lax.dot_general(
                    weights.astype(jnp.bfloat16),
                    v_buf[head],
                    (((1,), (0,)), ((), ())),
                    preferred_element_type=jnp.float32,
                )
                o_buf[head, token_rows(device), :] = (mixed / total).astype(jnp.bfloat16)

                @pl.when(device != me)
                def _():
                    pltpu.make_async_remote_copy(
                        src_ref=o_buf.at[head, token_rows(device)],
                        dst_ref=out_ref.at[:, columns(me, head)],
                        send_sem=o_send_sem,
                        recv_sem=o_sem,
                        device_id={"seq": device},
                        device_id_type=MESH,
                    ).start()

                @pl.when(device == me)
                def _():
                    pltpu.make_async_copy(
                        o_buf.at[head, token_rows(device)],
                        out_ref.at[:, columns(me, head)],
                        o_sem,
                    ).start()

            return carry

        lax.fori_loop(0, chips, attend, 0)

    sent = pl.ds(0, (n - 1) * rows)
    for head in range(per):
        for t in range(3):
            pltpu.make_async_copy(
                k_buf.at[head, sent], k_buf.at[head, sent], send_sem.at[head, t]
            ).wait()
    all_sent = o_buf.at[:, sent]
    pltpu.make_async_copy(all_sent, all_sent, o_send_sem).wait()
    pltpu.make_async_copy(out_ref, out_ref, o_sem).wait()


def local(queries, keys_in, value_input, head_class, block_lists):
    n = lax.axis_size("seq")
    rows, width = queries.shape
    heads = head_class.shape[0]
    per = heads // n
    head_dim = width // heads
    tokens = n * rows
    blocks = tokens // BLOCK_LEN
    hbm = pl.BlockSpec(memory_space=pltpu.HBM)
    buffer = pltpu.VMEM((per, tokens, head_dim), jnp.bfloat16)
    return pl.pallas_call(
        functools.partial(kernel, n, per, head_dim),
        out_shape=pltpu.VMEM((rows, width), jnp.bfloat16),
        in_specs=[hbm] * 5,
        out_specs=pl.BlockSpec(memory_space=pltpu.VMEM),
        scratch_shapes=[
            buffer,
            buffer,
            buffer,
            buffer,
            pltpu.VMEM((per, blocks, tokens), jnp.float32),
            pltpu.SMEM((heads,), jnp.int32),
            pltpu.VMEM(block_lists.shape[1:] + (heads,), jnp.int32),
            pltpu.SemaphoreType.REGULAR,
            pltpu.SemaphoreType.REGULAR((2, n // 4 - 1)),
            pltpu.SemaphoreType.DMA((2,)),
            pltpu.SemaphoreType.DMA((per, 3)),
            pltpu.SemaphoreType.DMA((per, 2)),
            pltpu.SemaphoreType.DMA((per, n)),
            pltpu.SemaphoreType.DMA,
            pltpu.SemaphoreType.DMA,
        ],
        compiler_params=pltpu.CompilerParams(
            collective_id=0, has_side_effects=True, vmem_limit_bytes=48 << 20
        ),
        cost_estimate=pl.CostEstimate(
            flops=4 * per * tokens * tokens * head_dim,
            bytes_accessed=8 * rows * width,
            transcendentals=per * tokens * tokens,
        ),
    )(
        *(
            pltpu.with_memory_space_constraint(x, pltpu.HBM)
            for x in (queries, keys_in, value_input, head_class, jnp.transpose(block_lists, (1, 2, 0)))
        )
    )


def solution(mesh):
    placed = (
        P(("clip", "seq"), None),
        P(("clip", "seq"), None),
        P(("clip", "seq"), None),
        P("clip"),
        P("clip", None, None),
    )
    return jax.shard_map(
        local, mesh=mesh, in_specs=placed, out_specs=P(("clip", "seq"), None), check_vma=False
    )
```

```python
import functools
import math

import jax
import jax.numpy as jnp
from jax import lax
from jax.experimental import pallas as pl
from jax.experimental.pallas import tpu as pltpu
from jax.sharding import PartitionSpec as P

MESH = pl.DeviceIdType.MESH
BLOCK_LEN = 128
EARLY = (0,)


def ring_delta(step):
    return (2 * (step % 2) - 1) * ((step + 1) // 2)


def service(chip, step, chips):
    out = EARLY[0]
    for k in range(1, len(EARLY)):
        out = jnp.where(step == k, EARLY[k], out)
    seen = len(EARLY)
    for k in range(chips):
        other = lax.rem(chip + 2 * chips - ring_delta(chips - 1 - k), chips)
        fresh = other >= 0
        for e in EARLY:
            fresh = jnp.logical_and(fresh, other != e)
        out = jnp.where(jnp.logical_and(fresh, step == seen), other, out)
        seen = seen + fresh.astype(jnp.int32)
    return out


def kernel(
    n, per, head_dim, q_ref, k_ref, v_ref, class_ref, lists_ref, out_ref,
    q_buf, k_buf, v_buf, o_buf, bias, class_mem, lists_mem,
    late_sem, wave_sem, small_sem, send_sem, kv_sem, q_sem, o_send_sem, o_sem,
):
    me = lax.axis_index("seq")
    chips = n // 2
    chip, core = me // 2, me % 2
    rows = q_ref.shape[0]
    tokens = n * rows
    blocks = tokens // BLOCK_LEN

    def columns(device, head):
        return pl.ds(pl.multiple_of((device * per + head) * head_dim, head_dim), head_dim)

    def token_rows(device):
        return pl.ds(pl.multiple_of(device * rows, rows), rows)

    def tensors(head, target_row):
        return (
            (k_ref, k_buf, kv_sem.at[head, 0]),
            (v_ref, v_buf, kv_sem.at[head, 1]),
            (q_ref, q_buf, q_sem.at[head, target_row]),
        )

    barrier = pltpu.get_barrier_semaphore()
    has_late = lax.axis_index("clip") == 0
    is_late = jnp.logical_and(has_late, me == 0)
    on_time = jnp.logical_not(is_late)

    def at(distance, which):
        return lax.rem(chip + chips + distance, chips) * 2 + which

    def signal(sem, target):
        pl.semaphore_signal(sem, inc=1, device_id={"seq": target}, device_id_type=MESH)

    near = (at(0, 1 - core), at(1, 0), at(1, 1), at(-1, 0), at(-1, 1))

    @pl.when(on_time)
    def _():
        for target in near:
            signal(barrier, target)

    @pl.when(jnp.logical_and(has_late, jnp.logical_and(chip > 1, chip < chips - 1)))
    def _():
        signal(barrier, 0)

    class_copy = pltpu.make_async_copy(class_ref, class_mem, small_sem.at[0])
    class_copy.start()
    lists_copy = pltpu.make_async_copy(lists_ref, lists_mem, small_sem.at[1])
    lists_copy.start()

    for head in range(per):
        for src, buf, sem in tensors(head, me):
            pltpu.make_async_copy(
                src.at[:, columns(me, head)], buf.at[head, token_rows(me)], sem
            ).start()

    beside_late = jnp.logical_and(has_late, jnp.logical_or(chip <= 1, chip == chips - 1))
    few = jnp.where(beside_late, len(near) - 1, len(near))
    pl.semaphore_wait(barrier, jnp.where(is_late, n - 1, few))

    def answer(d, carry):
        signal(late_sem, lax.rem(me + d, n))
        return carry

    @pl.when(is_late)
    def _():
        lax.fori_loop(1, n, answer, 0)

    def unless_late(target, act):
        pl.when(jnp.logical_not(jnp.logical_and(has_late, target == 0)))(act)

    def tell(side, wave):
        for which in range(2):
            target = at(side, which)
            unless_late(target, lambda: signal(wave_sem.at[(1 - side) // 2, wave - 2], target))

    def hear(side, wave):
        told = jnp.where(jnp.logical_and(has_late, at(side, 0) == 0), 1, 2)
        pl.semaphore_wait(wave_sem.at[(1 + side) // 2, wave - 2], told)

    def send(target, head):
        for t, (src, buf, sem) in enumerate(tensors(head, me)):
            pltpu.make_async_remote_copy(
                src_ref=src.at[:, columns(target, head)],
                dst_ref=buf.at[head, token_rows(me)],
                send_sem=send_sem.at[head, t],
                recv_sem=sem,
                device_id={"seq": target},
                device_id_type=MESH,
            ).start()

    def send_first(distance):
        def one(which, carry):
            target = at(distance, which)
            unless_late(target, lambda: send(target, 0))
            return carry

        lax.fori_loop(0, 2, one, 0)

    @pl.when(on_time)
    def _():
        tell(-1, 2)
        tell(1, 2)

    unless_late(near[0], lambda: send(near[0], 0))
    send_first(1)
    send_first(-1)
    for wave in range(2, chips // 2 + 1):

        @pl.when(on_time)
        def _():
            hear(1, wave)
            if wave < chips // 2:
                tell(-1, wave + 1)
                hear(-1, wave)
            if wave + 1 < chips // 2:
                tell(1, wave + 1)

        send_first(wave)
        if wave < chips // 2:
            send_first(-wave)

    @pl.when(jnp.logical_and(has_late, me > 0))
    def _():
        pl.semaphore_wait(late_sem, 1)
        send(0, 0)

    def peer(i):
        target_chip = lax.rem(chip + chips + ring_delta((i + 1) // 2), chips)
        return target_chip * 2 + (core + (i + 1) % 2) % 2

    def later_head(i, carry, head):
        send(peer(i), head)
        return carry

    for head in range(1, per):
        lax.fori_loop(0, n - 1, functools.partial(later_head, head=head), 0)

    class_copy.wait()
    lists_copy.wait()
    key_block = lax.broadcasted_iota(jnp.int32, (blocks, tokens), 1) // BLOCK_LEN
    lists = lists_mem[...].astype(jnp.float32)
    head_lane = lax.broadcasted_iota(jnp.int32, (blocks, lists.shape[2]), 1)
    for head in range(per):
        mine = head_lane == me * per + head
        allowed = None
        for j in range(lists.shape[1]):
            listed = jnp.sum(jnp.where(mine, lists[:, j, :], 0.0), axis=1, keepdims=True)
            hit = listed.astype(jnp.int32) == key_block
            allowed = hit if allowed is None else jnp.logical_or(allowed, hit)
        closed = jnp.where(class_mem[me * per + head] == 1, 0.0, -jnp.inf)
        bias[head] = jnp.where(allowed, 0.0, closed)

    factor = math.log2(math.e) / math.sqrt(head_dim)

    for head in range(per):
        pltpu.make_async_copy(k_buf.at[head], k_buf.at[head], kv_sem.at[head, 0]).wait()
        pltpu.make_async_copy(v_buf.at[head], v_buf.at[head], kv_sem.at[head, 1]).wait()

        def attend(step, carry, head=head):
            source_chip = service(chip, step, chips)
            for half in range(2):
                device = source_chip * 2 + half
                pltpu.make_async_copy(
                    q_buf.at[head, token_rows(device)],
                    q_buf.at[head, token_rows(device)],
                    q_sem.at[head, device],
                ).wait()
            pair_rows = pl.ds(pl.multiple_of(source_chip * 2 * rows, 2 * rows), 2 * rows)
            scores = lax.dot_general(
                q_buf[head, pair_rows, :],
                k_buf[head],
                (((1,), (1,)), ((), ())),
                preferred_element_type=jnp.float32,
            )
            for half in (1, 0) if head % 2 else (0, 1):
                device = source_chip * 2 + half
                part = scores[half * rows : (half + 1) * rows] + bias[head, pl.ds(device, 1), :]
                largest = jnp.max(part, axis=1, keepdims=True)
                weights = jnp.exp2((part - largest) * factor)
                total = jnp.sum(weights, axis=1, keepdims=True)
                mixed = lax.dot_general(
                    weights.astype(jnp.bfloat16),
                    v_buf[head],
                    (((1,), (0,)), ((), ())),
                    preferred_element_type=jnp.float32,
                )
                o_buf[head, token_rows(device), :] = (mixed / total).astype(jnp.bfloat16)

                @pl.when(device != me)
                def _():
                    pltpu.make_async_remote_copy(
                        src_ref=o_buf.at[head, token_rows(device)],
                        dst_ref=out_ref.at[:, columns(me, head)],
                        send_sem=o_send_sem,
                        recv_sem=o_sem,
                        device_id={"seq": device},
                        device_id_type=MESH,
                    ).start()

                @pl.when(device == me)
                def _():
                    pltpu.make_async_copy(
                        o_buf.at[head, token_rows(device)],
                        out_ref.at[:, columns(me, head)],
                        o_sem,
                    ).start()

            return carry

        lax.fori_loop(0, chips, attend, 0)

    sent = pl.ds(0, (n - 1) * rows)
    for head in range(per):
        for t in range(3):
            pltpu.make_async_copy(
                k_buf.at[head, sent], k_buf.at[head, sent], send_sem.at[head, t]
            ).wait()
    all_sent = o_buf.at[:, sent]
    pltpu.make_async_copy(all_sent, all_sent, o_send_sem).wait()
    pltpu.make_async_copy(out_ref, out_ref, o_sem).wait()


def local(queries, keys_in, value_input, head_class, block_lists):
    n = lax.axis_size("seq")
    rows, width = queries.shape
    heads = head_class.shape[0]
    per = heads // n
    head_dim = width // heads
    tokens = n * rows
    blocks = tokens // BLOCK_LEN
    hbm = pl.BlockSpec(memory_space=pltpu.HBM)
    buffer = pltpu.VMEM((per, tokens, head_dim), jnp.bfloat16)
    return pl.pallas_call(
        functools.partial(kernel, n, per, head_dim),
        out_shape=pltpu.VMEM((rows, width), jnp.bfloat16),
        in_specs=[hbm] * 5,
        out_specs=pl.BlockSpec(memory_space=pltpu.VMEM),
        scratch_shapes=[
            buffer,
            buffer,
            buffer,
            buffer,
            pltpu.VMEM((per, blocks, tokens), jnp.float32),
            pltpu.SMEM((heads,), jnp.int32),
            pltpu.VMEM(block_lists.shape[1:] + (heads,), jnp.int32),
            pltpu.SemaphoreType.REGULAR,
            pltpu.SemaphoreType.REGULAR((2, n // 4 - 1)),
            pltpu.SemaphoreType.DMA((2,)),
            pltpu.SemaphoreType.DMA((per, 3)),
            pltpu.SemaphoreType.DMA((per, 2)),
            pltpu.SemaphoreType.DMA((per, n)),
            pltpu.SemaphoreType.DMA,
            pltpu.SemaphoreType.DMA,
        ],
        compiler_params=pltpu.CompilerParams(
            collective_id=0, has_side_effects=True, vmem_limit_bytes=48 << 20
        ),
        cost_estimate=pl.CostEstimate(
            flops=4 * per * tokens * tokens * head_dim,
            bytes_accessed=8 * rows * width,
            transcendentals=per * tokens * tokens,
        ),
    )(
        *(
            pltpu.with_memory_space_constraint(x, pltpu.HBM)
            for x in (queries, keys_in, value_input, head_class, jnp.transpose(block_lists, (1, 2, 0)))
        )
    )


def solution(mesh):
    placed = (
        P(("clip", "seq"), None),
        P(("clip", "seq"), None),
        P(("clip", "seq"), None),
        P("clip"),
        P("clip", None, None),
    )
    return jax.shard_map(
        local, mesh=mesh, in_specs=placed, out_specs=P(("clip", "seq"), None), check_vma=False
    )
```

```python
import functools
import math

import jax
import jax.numpy as jnp
from jax import lax
from jax.experimental import pallas as pl
from jax.experimental.pallas import tpu as pltpu
from jax.sharding import PartitionSpec as P

MESH = pl.DeviceIdType.MESH
BLOCK_LEN = 128
EARLY = (0,)


def ring_delta(step):
    return (2 * (step % 2) - 1) * ((step + 1) // 2)


def service(chip, step, chips):
    out = EARLY[0]
    for k in range(1, len(EARLY)):
        out = jnp.where(step == k, EARLY[k], out)
    seen = len(EARLY)
    for k in range(chips):
        other = lax.rem(chip + 2 * chips - ring_delta(chips - 1 - k), chips)
        fresh = other >= 0
        for e in EARLY:
            fresh = jnp.logical_and(fresh, other != e)
        out = jnp.where(jnp.logical_and(fresh, step == seen), other, out)
        seen = seen + fresh.astype(jnp.int32)
    return out


def kernel(
    n, per, head_dim, q_ref, k_ref, v_ref, class_ref, lists_ref, out_ref,
    q_buf, k_buf, v_buf, o_buf, bias, class_mem, lists_mem,
    late_sem, wave_sem, small_sem, send_sem, kv_sem, q_sem, o_send_sem, o_sem,
):
    me = lax.axis_index("seq")
    chips = n // 2
    chip, core = me // 2, me % 2
    rows = q_ref.shape[0]
    tokens = n * rows
    blocks = tokens // BLOCK_LEN

    def columns(device, head):
        return pl.ds(pl.multiple_of((device * per + head) * head_dim, head_dim), head_dim)

    def token_rows(device):
        return pl.ds(pl.multiple_of(device * rows, rows), rows)

    def tensors(head, target_row):
        return (
            (k_ref, k_buf, kv_sem.at[head, 0]),
            (v_ref, v_buf, kv_sem.at[head, 1]),
            (q_ref, q_buf, q_sem.at[head, target_row]),
        )

    barrier = pltpu.get_barrier_semaphore()
    has_late = lax.axis_index("clip") == 0
    is_late = jnp.logical_and(has_late, me == 0)
    on_time = jnp.logical_not(is_late)

    def at(distance, which):
        return lax.rem(chip + chips + distance, chips) * 2 + which

    def signal(sem, target):
        pl.semaphore_signal(sem, inc=1, device_id={"seq": target}, device_id_type=MESH)

    near = (at(0, 1 - core), at(1, 0), at(1, 1), at(-1, 0), at(-1, 1))

    @pl.when(on_time)
    def _():
        for target in near:
            signal(barrier, target)

    @pl.when(jnp.logical_and(has_late, jnp.logical_and(chip > 1, chip < chips - 1)))
    def _():
        signal(barrier, 0)

    class_copy = pltpu.make_async_copy(class_ref, class_mem, small_sem.at[0])
    class_copy.start()
    lists_copy = pltpu.make_async_copy(lists_ref, lists_mem, small_sem.at[1])
    lists_copy.start()

    for head in range(per):
        for src, buf, sem in tensors(head, me):
            pltpu.make_async_copy(
                src.at[:, columns(me, head)], buf.at[head, token_rows(me)], sem
            ).start()

    beside_late = jnp.logical_and(has_late, jnp.logical_or(chip <= 1, chip == chips - 1))
    few = jnp.where(beside_late, len(near) - 1, len(near))
    pl.semaphore_wait(barrier, jnp.where(is_late, n - 1, few))

    def answer(d, carry):
        signal(late_sem, lax.rem(me + d, n))
        return carry

    @pl.when(is_late)
    def _():
        lax.fori_loop(1, n, answer, 0)

    def unless_late(target, act):
        pl.when(jnp.logical_not(jnp.logical_and(has_late, target == 0)))(act)

    def tell(side, wave):
        for which in range(2):
            target = at(side, which)
            unless_late(target, lambda: signal(wave_sem.at[(1 - side) // 2, wave - 2], target))

    def hear(side, wave):
        told = jnp.where(jnp.logical_and(has_late, at(side, 0) == 0), 1, 2)
        pl.semaphore_wait(wave_sem.at[(1 + side) // 2, wave - 2], told)

    def send(target, head):
        for t, (src, buf, sem) in enumerate(tensors(head, me)):
            pltpu.make_async_remote_copy(
                src_ref=src.at[:, columns(target, head)],
                dst_ref=buf.at[head, token_rows(me)],
                send_sem=send_sem.at[head, t],
                recv_sem=sem,
                device_id={"seq": target},
                device_id_type=MESH,
            ).start()

    def send_first(distance):
        def one(which, carry):
            target = at(distance, which)
            unless_late(target, lambda: send(target, 0))
            return carry

        lax.fori_loop(0, 2, one, 0)

    @pl.when(on_time)
    def _():
        tell(-1, 2)
        tell(1, 2)

    unless_late(near[0], lambda: send(near[0], 0))
    send_first(1)
    send_first(-1)
    for wave in range(2, chips // 2 + 1):

        @pl.when(on_time)
        def _():
            hear(1, wave)
            if wave < chips // 2:
                tell(-1, wave + 1)
                hear(-1, wave)
            if wave + 1 < chips // 2:
                tell(1, wave + 1)

        send_first(wave)
        if wave < chips // 2:
            send_first(-wave)

    @pl.when(jnp.logical_and(has_late, me > 0))
    def _():
        pl.semaphore_wait(late_sem, 1)
        send(0, 0)

    def peer(i):
        target_chip = lax.rem(chip + chips + ring_delta((i + 1) // 2), chips)
        return target_chip * 2 + (core + (i + 1) % 2) % 2

    def later_head(i, carry, head):
        send(peer(i), head)
        return carry

    for head in range(1, per):
        lax.fori_loop(0, n - 1, functools.partial(later_head, head=head), 0)

    class_copy.wait()
    lists_copy.wait()
    key_block = lax.broadcasted_iota(jnp.int32, (blocks, tokens), 1) // BLOCK_LEN
    lists = lists_mem[...].astype(jnp.float32)
    head_lane = lax.broadcasted_iota(jnp.int32, (blocks, lists.shape[2]), 1)
    for head in range(per):
        mine = head_lane == me * per + head
        allowed = None
        for j in range(lists.shape[1]):
            listed = jnp.sum(jnp.where(mine, lists[:, j, :], 0.0), axis=1, keepdims=True)
            hit = listed.astype(jnp.int32) == key_block
            allowed = hit if allowed is None else jnp.logical_or(allowed, hit)
        closed = jnp.where(class_mem[me * per + head] == 1, 0.0, -jnp.inf)
        bias[head] = jnp.where(allowed, 0.0, closed)

    factor = math.log2(math.e) / math.sqrt(head_dim)

    for head in range(per):
        pltpu.make_async_copy(k_buf.at[head], k_buf.at[head], kv_sem.at[head, 0]).wait()
        pltpu.make_async_copy(v_buf.at[head], v_buf.at[head], kv_sem.at[head, 1]).wait()

        def attend(step, carry, head=head):
            source_chip = service(chip, step, chips) if head else lax.rem(chip + chips - ring_delta(step), chips)
            for half in range(2):
                device = source_chip * 2 + half
                pltpu.make_async_copy(
                    q_buf.at[head, token_rows(device)],
                    q_buf.at[head, token_rows(device)],
                    q_sem.at[head, device],
                ).wait()
            pair_rows = pl.ds(pl.multiple_of(source_chip * 2 * rows, 2 * rows), 2 * rows)
            scores = lax.dot_general(
                q_buf[head, pair_rows, :],
                k_buf[head],
                (((1,), (1,)), ((), ())),
                preferred_element_type=jnp.float32,
            )
            for half in (1, 0) if head % 2 else (0, 1):
                device = source_chip * 2 + half
                part = scores[half * rows : (half + 1) * rows] + bias[head, pl.ds(device, 1), :]
                largest = jnp.max(part, axis=1, keepdims=True)
                weights = jnp.exp2((part - largest) * factor)
                total = jnp.sum(weights, axis=1, keepdims=True)
                mixed = lax.dot_general(
                    weights.astype(jnp.bfloat16),
                    v_buf[head],
                    (((1,), (0,)), ((), ())),
                    preferred_element_type=jnp.float32,
                )
                o_buf[head, token_rows(device), :] = (mixed / total).astype(jnp.bfloat16)

                @pl.when(device != me)
                def _():
                    pltpu.make_async_remote_copy(
                        src_ref=o_buf.at[head, token_rows(device)],
                        dst_ref=out_ref.at[:, columns(me, head)],
                        send_sem=o_send_sem,
                        recv_sem=o_sem,
                        device_id={"seq": device},
                        device_id_type=MESH,
                    ).start()

                @pl.when(device == me)
                def _():
                    pltpu.make_async_copy(
                        o_buf.at[head, token_rows(device)],
                        out_ref.at[:, columns(me, head)],
                        o_sem,
                    ).start()

            return carry

        lax.fori_loop(0, chips, attend, 0)

    sent = pl.ds(0, (n - 1) * rows)
    for head in range(per):
        for t in range(3):
            pltpu.make_async_copy(
                k_buf.at[head, sent], k_buf.at[head, sent], send_sem.at[head, t]
            ).wait()
    all_sent = o_buf.at[:, sent]
    pltpu.make_async_copy(all_sent, all_sent, o_send_sem).wait()
    pltpu.make_async_copy(out_ref, out_ref, o_sem).wait()


def local(queries, keys_in, value_input, head_class, block_lists):
    n = lax.axis_size("seq")
    rows, width = queries.shape
    heads = head_class.shape[0]
    per = heads // n
    head_dim = width // heads
    tokens = n * rows
    blocks = tokens // BLOCK_LEN
    hbm = pl.BlockSpec(memory_space=pltpu.HBM)
    buffer = pltpu.VMEM((per, tokens, head_dim), jnp.bfloat16)
    return pl.pallas_call(
        functools.partial(kernel, n, per, head_dim),
        out_shape=pltpu.VMEM((rows, width), jnp.bfloat16),
        in_specs=[hbm] * 5,
        out_specs=pl.BlockSpec(memory_space=pltpu.VMEM),
        scratch_shapes=[
            buffer,
            buffer,
            buffer,
            buffer,
            pltpu.VMEM((per, blocks, tokens), jnp.float32),
            pltpu.SMEM((heads,), jnp.int32),
            pltpu.VMEM(block_lists.shape[1:] + (heads,), jnp.int32),
            pltpu.SemaphoreType.REGULAR,
            pltpu.SemaphoreType.REGULAR((2, n // 4 - 1)),
            pltpu.SemaphoreType.DMA((2,)),
            pltpu.SemaphoreType.DMA((per, 3)),
            pltpu.SemaphoreType.DMA((per, 2)),
            pltpu.SemaphoreType.DMA((per, n)),
            pltpu.SemaphoreType.DMA,
            pltpu.SemaphoreType.DMA,
        ],
        compiler_params=pltpu.CompilerParams(
            collective_id=0, has_side_effects=True, vmem_limit_bytes=48 << 20
        ),
        cost_estimate=pl.CostEstimate(
            flops=4 * per * tokens * tokens * head_dim,
            bytes_accessed=8 * rows * width,
            transcendentals=per * tokens * tokens,
        ),
    )(
        *(
            pltpu.with_memory_space_constraint(x, pltpu.HBM)
            for x in (queries, keys_in, value_input, head_class, jnp.transpose(block_lists, (1, 2, 0)))
        )
    )


def solution(mesh):
    placed = (
        P(("clip", "seq"), None),
        P(("clip", "seq"), None),
        P(("clip", "seq"), None),
        P("clip"),
        P("clip", None, None),
    )
    return jax.shard_map(
        local, mesh=mesh, in_specs=placed, out_specs=P(("clip", "seq"), None), check_vma=False
    )
```
